128 devices in a mesh: dp: 4 (over y), expert: 32 (over x, z, core).
Axes of the slice: x: 4, y: 4, z: 4, core: 2. Of those that a mesh axis runs over, the one named last changes fastest.
Arguments:
- tokens: bfloat16 [16384, 2880], P(('dp', 'expert')), may hold values from -6 to 6
- cotangent: bfloat16 [16384, 2880], P(('dp', 'expert')), may hold values from -4 to 4
- route: int32 [16384, 4], P(('dp', 'expert')), may hold values from 0 to 63, all different within a row; in each aligned block of 128 rows (0 to 127, 128 to 255, ...) at most 16 rows name the same one
- combine: bfloat16 [16384, 4], P(('dp', 'expert')), may hold values from 0.049804688 to 0.59765625
- w_gate: bfloat16 [4, 32, 2880, 720], P('dp', 'expert'), may hold values from -0.109375 to 0.109375
- w_up: bfloat16 [4, 32, 2880, 720], P('dp', 'expert'), may hold values from -0.109375 to 0.109375
- w_down: bfloat16 [4, 32, 720, 2880], P('dp', 'expert'), may hold values from -0.15625 to 0.15625
Outputs:
- grad_tokens: bfloat16 [16384, 2880], P(('dp', 'expert'))
- grad_combine: float32 [16384, 4], P(('dp', 'expert'))
- grad_down: bfloat16 [4, 32, 720, 2880], P('dp', 'expert')
The draws below stay inside these ranges and needn't reach their ends.
Inputs may be any that keep to these rules, and one draw needn't show every extreme that they name: `route`: each row names 4 different experts; every expert is named by some row. Among the rows of one device no expert is named more than 16 times, and in every draw some expert is named exactly 16 times by the rows of some device.
All inputs are finite; a program needn't handle non-finite values.
Results may differ from the reference program's by a relative error of at most 0.0058.
Values may be sent and summed in bfloat16 or wider, within the bound.
No kernel may reach another device: no remote copies, remote signals or barrier semaphores. Data moves between devices by JAX's collectives and lax.ppermute only.
A program may use at most 192 MiB of HBM per device.

```python
import math
import jax
import jax.numpy as jnp
import numpy as np
from jax import lax

D = 2880
FF = 1440
FFH = 720
TOP = 4
TOK_DEV = 128
EXPERTS = 64
MOST = 16
TOKENS = 16384
N_DP = 4
N_EXPERT = 32


def steps_of(stream_key, extent, shards, smallest, top_value):
    level = 1.0
    for dim, blocks in shards:
        steps = jax.random.uniform(jax.random.fold_in(jax.random.fold_in(stream_key, 6), dim), (blocks,), jnp.float32, smallest / len(shards), top_value / len(shards))
        level = level * jnp.repeat(jnp.exp(steps), extent[dim] // blocks).reshape((-1,) + (1,) * (len(extent) - 1 - dim))
    return level


def shared_out(key, own, number, rows, amount, top, limit, skew):
    order = jax.random.permutation(key, amount)
    packed, common = portions_of(amount, rows * top, limit, skew, True), portions_of(amount, rows * top, limit, skew, False)
    places = jnp.arange(amount)

    def named(sizes, rotation):
        used = int((sizes > 0).sum())
        fixed = max(1, used // 4)
        passed = fixed + (places - fixed + rotation * (used - fixed)) % max(1, amount - fixed)
        return jnp.zeros((amount,), jnp.int32).at[order[jnp.where(places < fixed, places, passed)]].set(jnp.asarray(sizes, jnp.int32))

    sizes = jnp.where(number % 4 == 0, named(packed, number // 4), named(common, number - number // 4 - 1))
    mixed = jax.random.permutation(jax.random.fold_in(own, 3), amount)
    donor, taker = mixed[0:amount // 2 * 2:2], mixed[1:amount // 2 * 2:2]
    slack = jnp.minimum(sizes[donor] - 1, limit - sizes[taker]) // 2
    slack = jnp.where((donor == order[0]) | (taker == order[0]) | (sizes[taker] == 0), 0, jnp.maximum(slack, 0))
    passed = jax.random.randint(jax.random.fold_in(own, 4), (amount // 2,), 0, 1 << 20) % (slack + 1)
    sizes = sizes.at[donor].add(-passed).at[taker].add(passed)
    members = jnp.searchsorted(jnp.cumsum(sizes), jnp.arange(rows * top), side="right").astype(jnp.int32)
    grid = members.reshape(top, rows).T
    grid = grid[jax.random.permutation(jax.random.fold_in(own, 1), rows)]
    rotation = jax.random.randint(jax.random.fold_in(own, 2), (rows, 1), 0, top)
    return jnp.take_along_axis(grid, (jnp.arange(top)[None, :] + rotation) % top, axis=1)


def portions_of(amount, total, bound, slope, full):
    portions = [(1 << 20) // math.isqrt(rank ** slope) + 1 for rank in range(1, amount + 1)]
    largest = bound if full else min(bound, max(-(-total // amount), total * portions[0] // sum(portions)))
    least = 1 if total - largest >= amount - 1 else 0
    given, rest = [largest] + [least] * (amount - 1), total - largest - least * (amount - 1)
    while rest > 0:
        free = [i for i in range(1, amount) if given[i] < largest] or [i for i in range(1, amount) if given[i] < bound]
        pool, left = sum([portions[i] for i in free]), rest
        for i in free:
            addition = min(bound - given[i], max(1, left * portions[i] // pool), rest)
            given[i] = given[i] + addition
            rest = rest - addition
    return np.array(given)


def bell_draw(key, extent, scale, limit, cuts=(), kind=jnp.bfloat16):
    entries = scale * jax.random.normal(key, extent, jnp.float32)
    if cuts:
        entries = entries * steps_of(key, extent, cuts, -0.22, 0.18)
    return jnp.clip(entries, -limit, limit).astype(kind)


def setup_inputs(seed: int = 0) -> dict:
    splits = jax.random.split(jax.random.key(seed), 8)
    tokens = bell_draw(splits[0], (TOKENS, D), 1.0, 6.0, ((0, 128),))
    cotangent = bell_draw(splits[1], (TOKENS, D), 0.5, 4.0, ((0, 128),))
    route_keys = jax.random.split(jax.random.fold_in(splits[2], 1), TOKENS // TOK_DEV)
    route_turns = jax.random.permutation(jax.random.fold_in(splits[2], 3), TOKENS // TOK_DEV)
    route = jax.vmap(lambda own, number: shared_out(jax.random.fold_in(splits[2], 2), own, number, TOK_DEV, EXPERTS, TOP, MOST, 1))(route_keys, route_turns).reshape((TOKENS, TOP))
    combine = jnp.clip(0.049804688 + 0.54785156 * jax.random.uniform(splits[3], (TOKENS, TOP), jnp.float32) ** steps_of(splits[3], (TOKENS, TOP), ((0, 128),), -0.2, 0.2), 0.049804688, 0.59765625).astype(jnp.bfloat16)
    w_gate = bell_draw(splits[4], (N_DP, N_EXPERT, D, FFH), D ** -0.5, 0.109375, ((0, 4), (1, 32)))
    w_up = bell_draw(splits[5], (N_DP, N_EXPERT, D, FFH), D ** -0.5, 0.109375, ((0, 4), (1, 32)))
    w_down = bell_draw(splits[6], (N_DP, N_EXPERT, FFH, D), FF ** -0.5, 0.15625, ((0, 4), (1, 32)))
    return dict(tokens=tokens, cotangent=cotangent, route=route, combine=combine, w_gate=w_gate, w_up=w_up, w_down=w_down)


def half_backward(rows, cot_rows, weight_rows, gate_half, up_half, down_half):
    contract = (((1,), (1,)), ((), ()))
    pre_gate = jnp.dot(rows, gate_half, preferred_element_type=jnp.float32)
    pre_up = jnp.dot(rows, up_half, preferred_element_type=jnp.float32)
    sigma = jax.nn.sigmoid(1.702 * pre_gate)
    act = (pre_gate * sigma * (pre_up + 1.0)).astype(jnp.bfloat16)
    act_wide = lax.optimization_barrier(act).astype(jnp.float32)
    back = lax.dot_general(cot_rows, down_half, contract, preferred_element_type=jnp.float32)
    partial_combine = jnp.sum(back * act_wide, axis=1).astype(jnp.bfloat16)
    weighted = weight_rows[:, None] * back
    grad_gate = (weighted * (pre_up + 1.0) * (sigma + 1.702 * pre_gate * sigma * (1.0 - sigma))).astype(jnp.bfloat16)
    grad_up = (weighted * pre_gate * sigma).astype(jnp.bfloat16)
    partial_tokens = (lax.dot_general(grad_gate, gate_half, contract, preferred_element_type=jnp.float32)
                      + lax.dot_general(grad_up, up_half, contract, preferred_element_type=jnp.float32)).astype(jnp.bfloat16)
    scaled = (weight_rows[:, None] * cot_rows.astype(jnp.float32)).astype(jnp.bfloat16)
    return partial_tokens, partial_combine, act, scaled


def reference(tokens, cotangent, route, combine, w_gate, w_up, w_down):
    pair_count = TOKENS * TOP
    pair_expert = route.reshape(-1).astype(jnp.int32)
    onehot = (pair_expert[:, None] == jnp.arange(EXPERTS, dtype=jnp.int32)[None, :]).astype(jnp.int32)
    counts = jnp.sum(onehot, axis=0, dtype=jnp.int32)
    padded = (counts + 127) // 128 * 128
    padded_start = jnp.cumsum(padded, dtype=jnp.int32) - padded
    plain_start = jnp.cumsum(counts, dtype=jnp.int32) - counts
    arrange = jnp.argsort(pair_expert, stable=True).astype(jnp.int32)
    sorted_expert = pair_expert[arrange]
    position = padded_start[sorted_expert] + jnp.arange(pair_count, dtype=jnp.int32) - plain_start[sorted_expert]
    block_total = pair_count // 128 + EXPERTS
    source = jnp.full((block_total * 128,), -1, jnp.int32).at[position].set(arrange)
    block_begin = jnp.arange(block_total, dtype=jnp.int32) * 128
    block_expert = jnp.sum((padded_start[None, :] <= block_begin[:, None]).astype(jnp.int32), axis=1, dtype=jnp.int32) - 1
    flat_combine = combine.reshape(-1)
    zero_index = jnp.zeros((), jnp.int32)

    def one_block(carry, inputs):
        down_total, token_total, combine_total = carry
        rows_src, expert_id = inputs
        usable = rows_src >= 0
        safe = jnp.where(usable, rows_src, 0).astype(jnp.int32)
        token_id = safe // TOP
        rows = tokens[token_id]
        cot_rows = cotangent[token_id]
        weight_rows = jnp.where(usable, flat_combine[safe].astype(jnp.float32), jnp.float32(0.0))
        group = (expert_id // N_EXPERT).astype(jnp.int32)
        column = (expert_id % N_EXPERT).astype(jnp.int32)
        token_terms = jnp.zeros((128, D), jnp.float32)
        combine_terms = jnp.zeros((128,), jnp.float32)
        for half_index in range(2):
            slab = (2 * group + half_index).astype(jnp.int32)
            gate_half = w_gate[slab, column]
            up_half = w_up[slab, column]
            down_half = w_down[slab, column]
            partial_tokens, partial_combine, act, scaled = half_backward(rows, cot_rows, weight_rows, gate_half, up_half, down_half)
            token_terms = token_terms + partial_tokens.astype(jnp.float32)
            combine_terms = combine_terms + partial_combine.astype(jnp.float32)
            down_term = lax.dot_general(act, scaled, (((0,), (0,)), ((), ())), preferred_element_type=jnp.float32)
            current = lax.dynamic_slice(down_total, (slab, column, zero_index, zero_index), (1, 1, FFH, D))
            down_total = lax.dynamic_update_slice(down_total, current + down_term[None, None], (slab, column, zero_index, zero_index))
        token_total = token_total.at[token_id].add(jnp.where(usable[:, None], token_terms, jnp.float32(0.0)))
        combine_total = combine_total.at[safe].add(jnp.where(usable, combine_terms, jnp.float32(0.0)))
        return (down_total, token_total, combine_total), None

    start = (jnp.zeros((N_DP, N_EXPERT, FFH, D), jnp.float32), jnp.zeros((TOKENS, D), jnp.float32), jnp.zeros((pair_count,), jnp.float32))
    blocks_in = (source.reshape(block_total, 128), block_expert)
    (down_total, token_total, combine_total), unused = lax.scan(one_block, start, blocks_in)
    return token_total.astype(jnp.bfloat16), combine_total.reshape(TOKENS, TOP), down_total.astype(jnp.bfloat16)
```

```python
import functools

import jax
import jax.numpy as jnp
from jax import lax
from jax.experimental import pallas as pl
from jax.experimental.pallas import tpu as pltpu
from jax.sharding import PartitionSpec as P

LANES = 128
VMEM_LIMIT = 60 * 1024 * 1024


def round_up(value, unit):
    return (value + unit - 1) // unit * unit


def slots_of(route, experts, capacity):
    rows = route.shape[0]
    hot = route[:, :, None] == jnp.arange(experts, dtype=jnp.int32)[None, None, :]
    named = jnp.any(hot, axis=1).astype(jnp.bfloat16)
    earlier = jnp.tril(jnp.ones((rows, rows), jnp.bfloat16), -1)
    before = jnp.dot(earlier, named, preferred_element_type=jnp.float32)
    rank = jnp.sum(jnp.where(hot, before[:, None, :], 0.0), axis=2).astype(jnp.int32)
    return route * capacity + rank


def select_kernel(first, count, slot_ref, rows_ref, extra_ref, out_ref):
    top = slot_ref.shape[0]
    width = rows_ref.shape[1]
    base = first + pl.program_id(0) * count
    place = base + lax.broadcasted_iota(jnp.int32, (count, slot_ref.shape[1]), 0)
    picks = [(slot_ref[c : c + 1, :] == place) for c in range(top)]
    pick = picks[0]
    for c in range(1, top):
        pick = jnp.logical_or(pick, picks[c])
    pick = pick.astype(jnp.float32).astype(jnp.bfloat16)
    body = jnp.dot(pick, rows_ref[...], preferred_element_type=jnp.float32)
    tail = body[:, width - LANES :]
    for c in range(top):
        one = picks[c].astype(jnp.float32).astype(jnp.bfloat16)
        tail += jnp.dot(one, extra_ref[c], preferred_element_type=jnp.float32)
    body = body.astype(jnp.bfloat16)
    tail = tail.astype(jnp.bfloat16)
    for h in range(out_ref.shape[1]):
        out_ref[0, h, :, : width - LANES] = body[:, : width - LANES]
        out_ref[0, h, :, width - LANES :] = tail


def select(slot, rows, extra, groups, halves, count):
    width = rows.shape[1]
    return pl.pallas_call(
        functools.partial(select_kernel, 0, count),
        grid=(groups,),
        out_shape=jax.ShapeDtypeStruct((groups, halves, count, width), jnp.bfloat16),
        in_specs=[
            pl.BlockSpec(slot.shape, lambda g: (0, 0)),
            pl.BlockSpec(rows.shape, lambda g: (0, 0)),
            pl.BlockSpec(extra.shape, lambda g: (0, 0, 0)),
        ],
        out_specs=pl.BlockSpec((1, halves, count, width), lambda g: (g, 0, 0, 0)),
        compiler_params=pltpu.CompilerParams(vmem_limit_bytes=VMEM_LIMIT),
        name="select_rows",
    )(slot, rows, extra)


def expert_kernel(spare, rows_ref, cot_ref, gate_ref, up_ref, down_ref, out_ref, act_ref):
    contract = (((1,), (1,)), ((), ()))
    width = rows_ref.shape[1]
    rows = rows_ref[...]
    pre_gate = jnp.dot(rows, gate_ref[...], preferred_element_type=jnp.float32)
    pre_up = jnp.dot(rows, up_ref[...], preferred_element_type=jnp.float32)
    back = lax.dot_general(
        cot_ref[...], down_ref[...], contract, preferred_element_type=jnp.float32
    )
    lane = lax.broadcasted_iota(jnp.int32, (rows.shape[0], LANES), 1)
    extra = jnp.where(lane >= spare, rows_ref[:, width - LANES :].astype(jnp.float32), 0.0)
    weight = jnp.sum(extra, axis=1, keepdims=True)
    sigma = jax.nn.sigmoid(1.702 * pre_gate)
    gated = pre_gate * sigma
    act = (gated * (pre_up + 1.0)).astype(jnp.bfloat16)
    act_ref[...] = act
    combine = jnp.sum(back * act.astype(jnp.float32), axis=1, keepdims=True)
    weighted = weight * back
    grad_gate = (
        weighted * (pre_up + 1.0) * (sigma + 1.702 * gated * (1.0 - sigma))
    ).astype(jnp.bfloat16)
    grad_up = (weighted * gated).astype(jnp.bfloat16)
    total = lax.dot_general(
        grad_gate, gate_ref[...], contract, preferred_element_type=jnp.float32
    ) + lax.dot_general(grad_up, up_ref[...], contract, preferred_element_type=jnp.float32)
    out_ref[:, : width - LANES] = total[:, : width - LANES].astype(jnp.bfloat16)
    tail = jnp.where(lane >= spare, jnp.where(extra > 0.0, combine, 0.0), total[:, width - LANES :])
    out_ref[:, width - LANES :] = tail.astype(jnp.bfloat16)


def expert_block(rows, cot, gate, up, down, spare, tile):
    count, width = rows.shape
    hidden = gate.shape[1]
    whole = lambda i: (0, 0)
    flops = 2 * 5 * count * width * hidden
    return pl.pallas_call(
        functools.partial(expert_kernel, spare),
        grid=(count // tile,),
        out_shape=(
            jax.ShapeDtypeStruct((count, width), jnp.bfloat16),
            jax.ShapeDtypeStruct((count, hidden), jnp.bfloat16),
        ),
        in_specs=[
            pl.BlockSpec((tile, width), lambda i: (i, 0)),
            pl.BlockSpec((tile, width), lambda i: (i, 0)),
            pl.BlockSpec(gate.shape, whole, pipeline_mode=pl.Buffered(1)),
            pl.BlockSpec(up.shape, whole, pipeline_mode=pl.Buffered(1)),
            pl.BlockSpec(down.shape, whole, pipeline_mode=pl.Buffered(1)),
        ],
        out_specs=(
            pl.BlockSpec((tile, width), lambda i: (i, 0)),
            pl.BlockSpec((tile, hidden), lambda i: (i, 0)),
        ),
        compiler_params=pltpu.CompilerParams(vmem_limit_bytes=VMEM_LIMIT),
        cost_estimate=pl.CostEstimate(
            flops=flops, bytes_accessed=6 * count * width + 6 * width * hidden, transcendentals=0
        ),
        name="expert_block",
    )(rows, cot, gate, up, down)


def down_kernel(spare, act_ref, tail_ref, cot_ref, out_ref, total_ref):
    step = pl.program_id(0)

    @pl.when(step == 0)
    def _():
        total_ref[...] = jnp.zeros_like(total_ref)

    lane = lax.broadcasted_iota(jnp.int32, tail_ref.shape, 1)
    extra = jnp.where(lane >= spare, tail_ref[...].astype(jnp.float32), 0.0)
    weight = jnp.sum(extra, axis=1, keepdims=True)
    scaled = (weight * cot_ref[...].astype(jnp.float32)).astype(jnp.bfloat16)
    total_ref[...] += lax.dot_general(
        act_ref[...], scaled, (((0,), (0,)), ((), ())), preferred_element_type=jnp.float32
    )

    @pl.when(step == pl.num_programs(0) - 1)
    def _():
        out_ref[...] = total_ref[: out_ref.shape[0], : out_ref.shape[1]].astype(jnp.bfloat16)


def down_block(act, rows, cot, spare, tile, hidden, feature):
    count, width = rows.shape
    padded = act.shape[1]
    return pl.pallas_call(
        functools.partial(down_kernel, spare),
        grid=(count // tile,),
        out_shape=jax.ShapeDtypeStruct((hidden, feature), jnp.bfloat16),
        in_specs=[
            pl.BlockSpec((tile, padded), lambda i: (i, 0)),
            pl.BlockSpec((tile, LANES), lambda i: (i, width // LANES - 1)),
            pl.BlockSpec((tile, width), lambda i: (i, 0)),
        ],
        out_specs=pl.BlockSpec((hidden, feature), lambda i: (0, 0)),
        scratch_shapes=[pltpu.VMEM((padded, width), jnp.float32)],
        compiler_params=pltpu.CompilerParams(vmem_limit_bytes=VMEM_LIMIT),
        cost_estimate=pl.CostEstimate(
            flops=2 * count * width * padded, bytes_accessed=2 * count * width, transcendentals=0
        ),
        name="down_block",
    )(act, rows, cot)


def gather_kernel(count, slot_ref, got_ref, token_ref, extra_ref, total_ref):
    step = pl.program_id(0)

    @pl.when(step == 0)
    def _():
        total_ref[...] = jnp.zeros_like(total_ref)

    top = slot_ref.shape[1]
    tokens = slot_ref.shape[0]
    width = got_ref.shape[2]
    base = step // 2 * count
    place = base + lax.broadcasted_iota(jnp.int32, (tokens, count), 1)
    pick = slot_ref[:, 0:1] == place
    for c in range(1, top):
        pick = jnp.logical_or(pick, slot_ref[:, c : c + 1] == place)
    pick = pick.astype(jnp.float32).astype(jnp.bfloat16)
    total_ref[...] += jnp.dot(pick, got_ref[0], preferred_element_type=jnp.float32)

    @pl.when(step == pl.num_programs(0) - 1)
    def _():
        token_ref[...] = total_ref[:, : token_ref.shape[1]].astype(jnp.bfloat16)
        extra_ref[...] = total_ref[:, width - LANES :]


def gather_sum(slot, got, feature):
    parts, count, width = got.shape
    tokens = slot.shape[0]
    return pl.pallas_call(
        functools.partial(gather_kernel, count),
        grid=(parts,),
        out_shape=(
            jax.ShapeDtypeStruct((tokens, feature), jnp.bfloat16),
            jax.ShapeDtypeStruct((tokens, LANES), jnp.float32),
        ),
        in_specs=[
            pl.BlockSpec(slot.shape, lambda i: (0, 0)),
            pl.BlockSpec((1, count, width), lambda i: (i, 0, 0)),
        ],
        out_specs=(
            pl.BlockSpec((tokens, feature), lambda i: (0, 0)),
            pl.BlockSpec((tokens, LANES), lambda i: (0, 0)),
        ),
        scratch_shapes=[pltpu.VMEM((tokens, width), jnp.float32)],
        compiler_params=pltpu.CompilerParams(vmem_limit_bytes=VMEM_LIMIT),
        name="gather_sum",
    )(slot, got)


def local(tokens, cotangent, route, combine, w_gate, w_up, w_down):
    dp_size = lax.axis_size("dp")
    col_size = lax.axis_size("expert")
    devices = dp_size * col_size
    tok_rows, feature = tokens.shape
    top = route.shape[1]
    experts = devices // 2
    capacity = 2 * tok_rows * top // experts
    hidden = w_gate.shape[3]
    width = round_up(feature + top, LANES)
    spare = feature - (width - LANES)
    wide = round_up(hidden, 256)
    gate = jnp.pad(w_gate[0, 0], ((0, width - feature), (0, wide - hidden)))
    up = jnp.pad(w_up[0, 0], ((0, width - feature), (0, wide - hidden)))
    down = jnp.pad(w_down[0, 0], ((0, wide - hidden), (0, width - feature)))
    slot = slots_of(route, experts, capacity)
    across = slot.T
    extra = jnp.zeros((top, tok_rows, LANES), jnp.bfloat16)
    for c in range(top):
        extra = extra.at[c, :, spare + c].set(combine[:, c])
    padding = ((0, 0), (0, width - feature))
    groups = dp_size // 2
    count = col_size * capacity

    def send(buffer):
        shaped = buffer.reshape(devices, capacity, width)
        got = lax.all_to_all(shaped, ("dp", "expert"), split_axis=0, concat_axis=0, tiled=True)
        return got.reshape(devices * capacity, width)

    rows = send(select(across, jnp.pad(tokens, padding), extra, groups, 2, count))
    cot = send(select(across, jnp.pad(cotangent, padding), jnp.zeros_like(extra), groups, 2, count))
    result, act = expert_block(rows, cot, gate, up, down, spare, 256)
    got = send(result)
    grad_down = down_block(act, rows, cot, spare, 512, hidden, feature)
    grad_tokens, tail = gather_sum(slot, got.reshape(dp_size, count, width), feature)
    grad_combine = tail[:, spare : spare + top]
    return grad_tokens, grad_combine, grad_down.reshape(1, 1, hidden, feature)


def solution(mesh):
    rows = P(("dp", "expert"), None)
    slab = P("dp", "expert", None, None)
    return jax.shard_map(
        local,
        mesh=mesh,
        in_specs=(rows, rows, rows, rows, slab, slab, slab),
        out_specs=(rows, rows, slab),
        check_vma=False,
    )
```

```python
import functools

import jax
import jax.numpy as jnp
from jax import lax
from jax.experimental import pallas as pl
from jax.experimental.pallas import tpu as pltpu
from jax.sharding import PartitionSpec as P

LANES = 128
VMEM_LIMIT = 60 * 1024 * 1024
TILE_ROWS = 256
QUICK = pl.CostEstimate(flops=1 << 20, bytes_accessed=1 << 20, transcendentals=0)


def round_up(value, unit):
    return (value + unit - 1) // unit * unit


def one_hot(cond):
    return cond.astype(jnp.float32).astype(jnp.bfloat16)


def picks_of(route, first, count, capacity, experts):
    top, tokens = route.shape
    expert = lax.broadcasted_iota(jnp.int32, (experts, tokens), 0)
    hot = [route[c : c + 1, :] == expert for c in range(top)]
    named = functools.reduce(jnp.logical_or, hot)
    row = lax.broadcasted_iota(jnp.int32, (tokens, tokens), 0)
    earlier = one_hot(row < lax.broadcasted_iota(jnp.int32, (tokens, tokens), 1))
    before = jnp.dot(one_hot(named), earlier, preferred_element_type=jnp.float32)
    place = lax.broadcasted_iota(jnp.int32, (count, tokens), 0)
    picks = []
    for c in range(top):
        rank = jnp.sum(jnp.where(hot[c], before, 0.0), axis=0, keepdims=True).astype(jnp.int32)
        picks.append(route[c : c + 1, :] * capacity + rank - first == place)
    return picks


def select_kernel(experts, spare, first_ref, route_ref, rows_ref, *refs):
    out_ref, padded_ref = refs[-2:]
    lines, _, capacity, width = out_ref.shape
    count = lines * capacity
    feature = rows_ref.shape[2]
    picks = picks_of(route_ref[0], first_ref[0], count, capacity, experts)
    padded_ref[:, width - LANES :] = jnp.zeros((padded_ref.shape[0], LANES), jnp.bfloat16)
    padded_ref[:, :feature] = rows_ref[0]
    pick = one_hot(functools.reduce(jnp.logical_or, picks))
    body = jnp.dot(pick, padded_ref[...], preferred_element_type=jnp.float32)
    if len(refs) == 3:
        tail = body[:, width - LANES :]
        lane = lax.broadcasted_iota(jnp.int32, tail.shape, 1)
        for c, one in enumerate(picks):
            weight = jnp.where(one, refs[0][c : c + 1, :].astype(jnp.float32), 0.0)
            tail = jnp.where(lane == spare + c, jnp.sum(weight, axis=1, keepdims=True), tail)
        tail = tail.astype(jnp.bfloat16).reshape(lines, capacity, LANES)
        body = body[:, : width - LANES].astype(jnp.bfloat16)
        out_ref[:, 0, :, : width - LANES] = body.reshape(lines, capacity, width - LANES)
        out_ref[:, 0, :, width - LANES :] = tail
    else:
        out_ref[:, 0] = body.astype(jnp.bfloat16).reshape(lines, capacity, width)


def select(first, route, rows, combine, lines, capacity, width, experts):
    groups, tokens, feature = rows.shape
    args = [first, route, rows]
    in_specs = [
        pl.BlockSpec(memory_space=pltpu.SMEM),
        pl.BlockSpec((1,) + route.shape[1:], lambda g: (g, 0, 0)),
        pl.BlockSpec((1, tokens, feature), lambda g: (g, 0, 0)),
    ]
    if combine is not None:
        args.append(combine)
        in_specs.append(pl.BlockSpec(combine.shape, lambda g: (0, 0)))
    return pl.pallas_call(
        functools.partial(select_kernel, experts, feature - (width - LANES)),
        grid=(groups,),
        out_shape=jax.ShapeDtypeStruct((lines, groups, capacity, width), jnp.bfloat16),
        in_specs=in_specs,
        out_specs=pl.BlockSpec((lines, 1, capacity, width), lambda g: (0, g, 0, 0)),
        scratch_shapes=[pltpu.VMEM((tokens, width), jnp.bfloat16)],
        compiler_params=pltpu.CompilerParams(vmem_limit_bytes=VMEM_LIMIT),
        cost_estimate=QUICK,
        name="select_rows",
    )(*args)


def hidden_kernel(rows_ref, gate_ref, up_ref, *refs):
    gate_out, up_out, tail_out = refs[-3:]
    contract = (((1,), (1,)), ((), ()))
    lines, _, capacity, width = rows_ref.shape
    rows = rows_ref[:, 0].reshape(lines * capacity, width)
    gate_out[0] = lax.dot_general(rows, gate_ref[...], contract, preferred_element_type=jnp.float32)
    up_out[0] = lax.dot_general(rows, up_ref[...], contract, preferred_element_type=jnp.float32)
    tail_out[0] = rows[:, width - LANES :]


def hidden_block(rows, gate, up, buffers, place, offset, classes, count):
    lines, _, capacity, width = rows.shape
    hidden = gate.shape[0]
    part = TILE_ROWS // capacity
    first = offset // TILE_ROWS
    whole = pl.BlockSpec((hidden, width), lambda i: (0, 0), pipeline_mode=pl.Buffered(1))
    shapes = (
        jax.ShapeDtypeStruct((classes, count, hidden), jnp.float32),
        jax.ShapeDtypeStruct((classes, count, hidden), jnp.float32),
        jax.ShapeDtypeStruct((classes, count, LANES), jnp.bfloat16),
    )
    held = [] if buffers is None else list(buffers)
    return pl.pallas_call(
        hidden_kernel,
        grid=(lines // part,),
        out_shape=shapes,
        in_specs=[pl.BlockSpec((part, 1, capacity, width), lambda i: (i, 0, 0, 0)), whole, whole]
        + [pl.BlockSpec(memory_space=pl.ANY)] * len(held),
        out_specs=tuple(
            pl.BlockSpec((1, TILE_ROWS, s.shape[2]), lambda i: (place, first + i, 0)) for s in shapes
        ),
        input_output_aliases={3 + i: i for i in range(len(held))},
        compiler_params=pltpu.CompilerParams(vmem_limit_bytes=VMEM_LIMIT),
        cost_estimate=QUICK,
        name="hidden_block",
    )(rows, gate, up, *held)


def expert_kernel(
    spare, gate_in, up_in, tail_in, cot_ref, gate_ref, up_ref, down_ref, out_ref, act_ref
):
    contract = (((1,), (1,)), ((), ()))
    lines, _, capacity, width = cot_ref.shape
    count = lines * capacity
    cot = cot_ref[:, 0].reshape(count, width)
    back = lax.dot_general(cot, down_ref[...], contract, preferred_element_type=jnp.float32)
    pre_gate = gate_in[0]
    pre_up = up_in[0]
    lane = lax.broadcasted_iota(jnp.int32, (count, LANES), 1)
    extra = jnp.where(lane >= spare, tail_in[0].astype(jnp.float32), 0.0)
    weight = jnp.sum(extra, axis=1, keepdims=True)
    sigma = jax.nn.sigmoid(1.702 * pre_gate)
    gated = pre_gate * sigma
    act = (gated * (pre_up + 1.0)).astype(jnp.bfloat16)
    act_ref[...] = act
    combine = jnp.sum(back * act.astype(jnp.float32), axis=1, keepdims=True)
    weighted = weight * back
    grad_gate = (
        weighted * (pre_up + 1.0) * (sigma + 1.702 * gated * (1.0 - sigma))
    ).astype(jnp.bfloat16)
    grad_up = (weighted * gated).astype(jnp.bfloat16)
    total = jnp.dot(grad_gate, gate_ref[...], preferred_element_type=jnp.float32) + jnp.dot(
        grad_up, up_ref[...], preferred_element_type=jnp.float32
    )
    out_ref[:, : width - LANES] = total[:, : width - LANES].astype(jnp.bfloat16)
    tail = jnp.where(lane >= spare, jnp.where(extra > 0.0, combine, 0.0), total[:, width - LANES :])
    out_ref[:, width - LANES :] = tail.astype(jnp.bfloat16)


def expert_block(hidden, place, cot, group, gate, up, down, spare):
    pre_gate, pre_up, tail = hidden
    lines, _, capacity, width = cot.shape
    count = lines * capacity
    size = gate.shape[0]
    part = TILE_ROWS // capacity
    whole = pl.BlockSpec((size, width), lambda i: (0, 0), pipeline_mode=pl.Buffered(1))
    held = lambda cols: pl.BlockSpec((1, TILE_ROWS, cols), lambda i: (place, i, 0))
    out = lambda cols: pl.BlockSpec((TILE_ROWS, cols), lambda i: (i, 0))
    return pl.pallas_call(
        functools.partial(expert_kernel, spare),
        grid=(count // TILE_ROWS,),
        out_shape=(
            jax.ShapeDtypeStruct((count, width), jnp.bfloat16),
            jax.ShapeDtypeStruct((count, size), jnp.bfloat16),
        ),
        in_specs=[
            held(size),
            held(size),
            held(LANES),
            pl.BlockSpec((part, 1, capacity, width), lambda i: (i, group, 0, 0)),
            whole,
            whole,
            whole,
        ],
        out_specs=(out(width), out(size)),
        compiler_params=pltpu.CompilerParams(vmem_limit_bytes=VMEM_LIMIT),
        cost_estimate=QUICK,
        name="expert_block",
    )(pre_gate, pre_up, tail, cot, gate, up, down)


def down_kernel(spare, *refs):
    out_ref, total_ref = refs[-2:]
    step = pl.program_id(0)
    parts = (len(refs) - 2) // 3

    @pl.when(step == 0)
    def _():
        total_ref[...] = jnp.zeros_like(total_ref)

    for part in range(parts):

        @pl.when(step == part)
        def _(part=part):
            act_ref, tail_ref, cot_ref = refs[3 * part : 3 * part + 3]
            lines, _, capacity, width = cot_ref.shape
            count = lines * capacity
            lane = lax.broadcasted_iota(jnp.int32, (count, LANES), 1)
            extra = jnp.where(lane >= spare, tail_ref[0].astype(jnp.float32), 0.0)
            weight = jnp.sum(extra, axis=1, keepdims=True)
            cot = cot_ref[:, 0].reshape(count, width)
            scaled = (weight * cot.astype(jnp.float32)).astype(jnp.bfloat16)
            total_ref[...] += lax.dot_general(
                act_ref[...], scaled, (((0,), (0,)), ((), ())), preferred_element_type=jnp.float32
            )

    @pl.when(step == parts - 1)
    def _():
        out_ref[...] = total_ref[: out_ref.shape[0], : out_ref.shape[1]].astype(jnp.bfloat16)


def down_block(parts, spare, hidden, feature):
    args, in_specs = [], []
    for act, tail, place, cot, group in parts:
        lines, _, capacity, width = cot.shape
        count, size = act.shape
        args += [act, tail, cot]
        once = pl.Buffered(1)
        in_specs += [
            pl.BlockSpec((count, size), lambda i: (0, 0), pipeline_mode=once),
            pl.BlockSpec(
                (1, count, LANES), lambda i, place=place: (place, 0, 0), pipeline_mode=once
            ),
            pl.BlockSpec(
                (lines, 1, capacity, width),
                lambda i, group=group: (0, group, 0, 0),
                pipeline_mode=once,
            ),
        ]
    return pl.pallas_call(
        functools.partial(down_kernel, spare),
        grid=(len(parts),),
        out_shape=jax.ShapeDtypeStruct((hidden, feature), jnp.bfloat16),
        in_specs=in_specs,
        out_specs=pl.BlockSpec((hidden, feature), lambda i: (0, 0)),
        scratch_shapes=[pltpu.VMEM((size, width), jnp.float32)],
        compiler_params=pltpu.CompilerParams(vmem_limit_bytes=VMEM_LIMIT),
        cost_estimate=QUICK,
        name="down_block",
    )(*args)


def token_sum_kernel(experts, first_ref, route_ref, got_ref, *refs):
    lines, _, capacity, width = got_ref.shape
    count = lines * capacity
    got = got_ref[:, 0].reshape(count, width)
    picks = picks_of(route_ref[...], first_ref[0], count, capacity, experts)
    pick = one_hot(functools.reduce(jnp.logical_or, picks))
    total = lax.dot_general(
        pick, got, (((0,), (0,)), ((), ())), preferred_element_type=jnp.float32
    )
    if len(refs) == 1:
        refs[0][...] = total.astype(refs[0].dtype)
    else:
        base_ref, token_ref, extra_ref = refs
        total += base_ref[...]
        token_ref[...] = total[:, : token_ref.shape[1]].astype(jnp.bfloat16)
        extra_ref[...] = total[:, width - LANES :]


def token_sum(first, route, got, experts, dtype=None, base=None, feature=None):
    top, tokens = route.shape
    lines, _, capacity, width = got.shape
    whole = lambda *shape: pl.BlockSpec(shape, lambda i: (0,) * len(shape))
    args = [first, route, got]
    in_specs = [
        pl.BlockSpec(memory_space=pltpu.SMEM),
        whole(top, tokens),
        whole(lines, 1, capacity, width),
    ]
    if base is None:
        out_shape = jax.ShapeDtypeStruct((tokens, width), dtype)
        out_specs = whole(tokens, width)
    else:
        args.append(base)
        in_specs.append(whole(tokens, width))
        out_shape = (
            jax.ShapeDtypeStruct((tokens, feature), jnp.bfloat16),
            jax.ShapeDtypeStruct((tokens, LANES), jnp.float32),
        )
        out_specs = (whole(tokens, feature), whole(tokens, LANES))
    return pl.pallas_call(
        functools.partial(token_sum_kernel, experts),
        grid=(1,),
        out_shape=out_shape,
        in_specs=in_specs,
        out_specs=out_specs,
        compiler_params=pltpu.CompilerParams(vmem_limit_bytes=VMEM_LIMIT),
        cost_estimate=QUICK,
        name="token_sum",
    )(*args)


def local(tokens, cotangent, route, combine, w_gate, w_up, w_down):
    dp_size = lax.axis_size("dp")
    lines = lax.axis_size("expert")
    experts = dp_size * lines // 2
    tok_rows, feature = tokens.shape
    top = route.shape[1]
    capacity = 2 * tok_rows * top // experts
    count = lines * capacity
    hidden = w_gate.shape[3]
    width = round_up(feature + top, LANES)
    spare = feature - (width - LANES)
    wide = round_up(hidden, 256)

    pair = [(i, i ^ 1) for i in range(dp_size)]
    cross = [(i, dp_size - 1 - i) for i in range(dp_size)]
    corner = [(i, i ^ 2) for i in range(dp_size)]

    def swap(value, moves):
        return lax.ppermute(value, "dp", moves)

    def exchange(buffer):
        shape = buffer.shape
        shaped = buffer.reshape(lines, -1, shape[-1])
        got = lax.all_to_all(shaped, "expert", split_axis=0, concat_axis=0, tiled=True)
        return got.reshape(shape)

    def after(value, *others):
        return lax.optimization_barrier((value,) + others)[0]

    own_first = (lax.axis_index("dp") // 2 * count).astype(jnp.int32).reshape(1)
    other_first = count - own_first
    pick_rows = lambda first, names, rows, weights: select(
        first, names, rows, weights, lines, capacity, width, experts
    )

    names = route.T
    weights = combine.T
    send_other = pick_rows(other_first, names[None], tokens[None], weights)
    send_own = pick_rows(own_first, names[None], tokens[None], weights)

    cot, place = after(cotangent, send_other), route
    cot_cross, cot_pair, cot_corner = swap(cot, cross), swap(cot, pair), swap(cot, corner)
    names_cross, names_pair, names_corner = (
        swap(place, cross).T,
        swap(place, pair).T,
        swap(place, corner).T,
    )
    send_cross = pick_rows(own_first, names_cross[None], cot_cross[None], None)
    send_pair = pick_rows(own_first, names_pair[None], cot_pair[None], None)
    send_last = pick_rows(
        own_first, jnp.stack([names_corner, names]), jnp.stack([cot_corner, cotangent]), None
    )

    padding = ((0, wide - hidden), (0, width - feature))
    gate = jnp.pad(w_gate[0, 0].T, padding)
    up = jnp.pad(w_up[0, 0].T, padding)
    down = jnp.pad(w_down[0, 0], padding)

    half = lines // 2
    first_half = count // 2
    rows_other = exchange(send_other)
    send_own = after(
        send_own, rows_other, cot_cross, cot_pair, cot_corner, gate, up, down,
        names_cross, names_pair, names_corner,
    )
    rows_own = exchange(send_own)
    cross_a = swap(rows_other[:half], cross)
    got_cross = exchange(after(send_cross, rows_own, cross_a, send_pair, send_last))
    cross_b = swap(rows_other[half:], cross)
    pair_a = swap(rows_own[:half], pair)
    held_two = hidden_block(rows_own, gate, up, None, 1, 0, 2, count)
    held_one = hidden_block(cross_a, gate, up, None, 0, 0, 2, count)
    got_pair = exchange(after(send_pair, got_cross, cross_b, pair_a, held_one[2], held_two[2]))
    pair_b = swap(rows_own[half:], pair)
    held_one = hidden_block(cross_b, gate, up, held_one, 0, first_half, 2, count)
    held_one = hidden_block(pair_a, gate, up, held_one, 1, 0, 2, count)
    result_cross, act_cross = expert_block(held_one, 0, got_cross, 0, gate, up, down, spare)
    got_last = exchange(after(send_last, got_pair, pair_b, act_cross))
    corner_a = swap(after(cross_a, pair_b), pair)
    corner_b = swap(after(cross_b, pair_b), pair)

    shape = (lines, 1, capacity, width)
    back_cross = swap(result_cross.reshape(shape), cross)
    held_one = hidden_block(pair_b, gate, up, held_one, 1, first_half, 2, count)
    result_pair, act_pair = expert_block(held_one, 1, got_pair, 0, gate, up, down, spare)
    back_pair = swap(result_pair, pair)
    corner_a, corner_b = after(corner_a, act_pair), after(corner_b, act_pair)
    held_two = hidden_block(corner_a, gate, up, held_two, 0, 0, 2, count)
    held_two = hidden_block(corner_b, gate, up, held_two, 0, first_half, 2, count)

    back_other = exchange(after(back_cross, got_last, act_pair, held_two[2]))
    result_corner, act_corner = expert_block(held_two, 0, got_last, 0, gate, up, down, spare)
    result_own, act_own = expert_block(held_two, 1, got_last, 1, gate, up, down, spare)
    back_corner = exchange(after(result_corner.reshape(shape), back_other))
    back_own = (result_own.astype(jnp.float32) + back_pair.astype(jnp.float32)).astype(jnp.bfloat16)
    back_own = exchange(after(back_own.reshape(shape), back_corner))

    sum_corner = token_sum(own_first, names_corner, back_corner, experts, dtype=jnp.bfloat16)
    sum_corner = swap(sum_corner, corner).astype(jnp.float32)
    total = token_sum(other_first, names, back_other, experts, dtype=jnp.float32) + sum_corner
    grad_down = down_block(
        (
            (act_cross, held_one[2], 0, got_cross, 0),
            (act_pair, held_one[2], 1, got_pair, 0),
            (after(act_corner, back_other), held_two[2], 0, got_last, 0),
            (act_own, held_two[2], 1, got_last, 1),
        ),
        spare,
        hidden,
        feature,
    )
    grad_tokens, tail = token_sum(
        own_first, names, back_own, experts, base=total, feature=feature
    )
    grad_combine = tail[:, spare : spare + top]
    return grad_tokens, grad_combine, grad_down.reshape(1, 1, hidden, feature)


def solution(mesh):
    rows = P(("dp", "expert"), None)
    slab = P("dp", "expert", None, None)
    return jax.shard_map(
        local,
        mesh=mesh,
        in_specs=(rows, rows, rows, rows, slab, slab, slab),
        out_specs=(rows, rows, slab),
        check_vma=False,
    )
```
